512 devices in a mesh: dp: 32 (over z, y_hi), layer: 16 (over y_lo, x, core).
Axes of the slice: x: 4, y: 4 (y_hi: 2, y_lo: 2; y = y_hi * 2 + y_lo), z: 16, core: 2. Of those that a mesh axis runs over, the one named last changes fastest.
Arguments:
- train_grads: float32 [4096, 16, 1024], P('dp', 'layer')
- query_grads: float32 [4096, 16, 1024], P('dp', 'layer'), may hold values from -6 to 6
- inverse_factors: float32 [16, 1024, 1024], P('layer', 'dp')
- repeat_counts: int32 [4096], P('dp'), may hold values from 1 to 4
Outputs:
- influence: float32 [4096, 1152], P(('dp', 'layer'))
The draws below stay inside these ranges and needn't reach their ends.
All inputs are finite; a program needn't handle non-finite values.
Results may differ from the reference program's by a relative error of at most 0.00014.
Values sent between devices are 32-bit elements; how exact they have to be, the bound alone decides.
No kernel may reach another device: no remote copies, remote signals or barrier semaphores. Data moves between devices by JAX's collectives and lax.ppermute only.
A program may use at most 64 MiB of HBM per device.

```python
import math
import jax
import jax.numpy as jnp
from jax import lax

P_SIZE = 1024
TDEV = 128
QDEV = 128
NTRAIN = 4096
NQ = 4096
NBLK = 16
N_DP = 32


def column_scales(key):
    return jnp.exp(jax.random.uniform(jax.random.fold_in(key, 11), (NBLK, P_SIZE), jnp.float32, math.log(0.3), math.log(3.0)))


def draw_train_grads(key, part):
    columns = column_scales(key)
    noise = jax.random.normal(jax.random.fold_in(key, 21), (NTRAIN, NBLK, P_SIZE), jnp.float32)
    row_scales = jnp.exp(jax.random.uniform(jax.random.fold_in(key, 22), (NTRAIN, 1, 1), jnp.float32, math.log(0.5), math.log(2.0)))
    return noise * row_scales * columns[None, :, :]


def draw_inverse_factors(key, part):
    columns = column_scales(key)
    spread = jax.random.uniform(jax.random.fold_in(key, 31), (NBLK, P_SIZE), jnp.float32, 0.6, 1.4)
    noise = jax.random.normal(jax.random.fold_in(key, 32), (NBLK, P_SIZE, P_SIZE), jnp.float32)
    diagonal = spread / (3.4 * columns * columns + 0.5)
    roots = jnp.sqrt(diagonal)
    rows_at = jax.lax.broadcasted_iota(jnp.int32, (P_SIZE, P_SIZE), 0)
    cols_at = jax.lax.broadcasted_iota(jnp.int32, (P_SIZE, P_SIZE), 1)
    on_diagonal = (rows_at == cols_at).astype(jnp.float32)[None, :, :]
    outside = noise * (0.2 / math.sqrt(P_SIZE)) * roots[:, :, None] * roots[:, None, :]
    return outside * (1.0 - on_diagonal) + on_diagonal * diagonal[:, :, None]


def place_ends(array, own_key, least, largest):
    index_at = [jax.random.randint(jax.random.fold_in(own_key, axis), (), 0, length) for axis, length in enumerate(array.shape)]
    main_axis = array.shape.index(max(array.shape))
    neighbour = index_at[:main_axis] + [(index_at[main_axis] + 1) % array.shape[main_axis]] + index_at[main_axis + 1:]
    return array.at[tuple(index_at)].set(least).at[tuple(neighbour)].set(largest)


def block_scale(own_key, dims, cuts, low, largest):
    gain = 1.0
    for position, blocks in cuts:
        steps = jax.random.uniform(jax.random.fold_in(jax.random.fold_in(own_key, 6), position), (blocks,), jnp.float32, low / len(cuts), largest / len(cuts))
        gain = gain * jnp.repeat(jnp.exp(steps), dims[position] // blocks).reshape((-1,) + (1,) * (len(dims) - 1 - position))
    return gain


def centred(stream_key, extent, scale, limit, split=(), kind=jnp.bfloat16):
    drawn = scale * jax.random.normal(stream_key, extent, jnp.float32)
    if split:
        drawn = drawn * block_scale(stream_key, extent, split, -0.22, 0.18)
    return jnp.clip(drawn, -limit, limit).astype(kind)


def setup_inputs(seed: int = 0) -> dict:
    streams_of = jax.random.split(jax.random.key(seed), 5)
    return {
        "train_grads": draw_train_grads(jax.random.fold_in(streams_of[4], 71), 0),
        "query_grads": centred(streams_of[1], (NQ, NBLK, P_SIZE), 1.0, 6.0, ((0, 32), (1, 16)), jnp.float32),
        "inverse_factors": draw_inverse_factors(jax.random.fold_in(streams_of[4], 71), 0),
        "repeat_counts": place_ends(jax.random.randint(streams_of[3], (NTRAIN,), 1, 5), jax.random.fold_in(streams_of[3], 1), 1, 4).astype(jnp.int32),
    }


DAMPING = 0.5
PRECISE = lax.Precision.HIGHEST

def reference(train_grads, query_grads, inverse_factors, repeat_counts):
    weights = repeat_counts.astype(jnp.float32)
    reach_steps = min(4, (N_DP - 1) // 2)
    window = 2 * reach_steps + 1
    score_scale = 1.0 / math.sqrt(P_SIZE * NBLK)

    def add_block(layer_index, scores):
        train = lax.dynamic_index_in_dim(train_grads, layer_index, 1, keepdims=False)
        query = lax.dynamic_index_in_dim(query_grads, layer_index, 1, keepdims=False)
        inverse = lax.dynamic_index_in_dim(inverse_factors, layer_index, 0, keepdims=False)
        fisher = jnp.dot((train * weights[:, None]).T, train, precision=PRECISE, preferred_element_type=jnp.float32)
        damped = fisher / NTRAIN + DAMPING * jnp.eye(P_SIZE, dtype=jnp.float32)
        first = jnp.dot(query, inverse.T, precision=PRECISE, preferred_element_type=jnp.float32)
        leftover = query - jnp.dot(first, damped, precision=PRECISE, preferred_element_type=jnp.float32)
        precond = first + jnp.dot(leftover, inverse.T, precision=PRECISE, preferred_element_type=jnp.float32)
        shards = precond.reshape(N_DP, QDEV, P_SIZE)
        windowed = jnp.stack([jnp.roll(shards, reach_steps - offset, axis=0) for offset in range(window)], axis=1)
        local_train = train.reshape(N_DP, TDEV, P_SIZE)
        return scores + jnp.einsum('dnp,dwmp->dnwm', local_train, windowed, precision=PRECISE)
    scores = lax.fori_loop(0, NBLK, add_block, jnp.zeros((N_DP, TDEV, window, QDEV), dtype=jnp.float32))
    scores = scores * (weights.reshape(N_DP, TDEV, 1, 1) * score_scale)
    return scores.reshape(NTRAIN, window * QDEV)
```

```python
import math

import jax
import jax.numpy as jnp
from jax import lax
from jax.sharding import Mesh, PartitionSpec as P

DAMPING = 0.5
FAST = lax.Precision.HIGH


def dot(left, right, dims):
    return lax.dot_general(
        left, right, (dims, ((), ())), precision=FAST, preferred_element_type=jnp.float32
    )


def shift_z(value, steps):
    count = lax.axis_size("z")
    return lax.ppermute(value, "z", [(i, (i + steps) % count) for i in range(count)])


def swap_y(value):
    return lax.ppermute(value, "yh", [(0, 1), (1, 0)])


def after(value, *others):
    return lax.optimization_barrier((value, *others))[0]


def reduce_near(blocks, place):
    def of_class(steps):
        return lax.dynamic_index_in_dim(blocks, (place + steps) % 4, 1, keepdims=False)

    opposite = of_class(2)
    from_left = shift_z(of_class(1), 1)
    from_right = shift_z(of_class(3), -1)
    from_left2 = shift_z(opposite[:, :8], 2)
    from_right2 = shift_z(opposite[:, 8:], -2)
    return of_class(0) + from_left + from_right + jnp.concatenate([from_left2, from_right2], axis=1)


def reduce_far(sums, place):
    row = place // 4

    def of_row(steps):
        return lax.dynamic_index_in_dim(sums, (row + steps) % 4, 0, keepdims=False)

    opposite = of_row(2)
    passing_right = shift_z(opposite[:8], 4)
    passing_left = shift_z(opposite[8:], -4)
    right, left = of_row(1), of_row(3)
    from_left = shift_z(jnp.concatenate([right[:8] + passing_right, right[8:]]), 4)
    from_right = shift_z(jnp.concatenate([left[:8], left[8:] + passing_left]), -4)
    return of_row(0) + from_left + from_right


def gather_far(part):
    plus4 = shift_z(part, -4)
    minus4 = shift_z(part, 4)
    plus8 = jnp.concatenate([shift_z(plus4[:8], -4), shift_z(minus4[8:], 4)])
    return jnp.stack([part, plus4, plus8, minus4])


def gather_near(parts):
    plus1 = shift_z(parts, -1)
    minus1 = shift_z(parts, 1)
    plus2 = shift_z(parts[:, :8], -2)
    minus2 = shift_z(parts[:, 8:], 2)
    two = jnp.concatenate([plus2, jnp.roll(minus2, -1, axis=0)], axis=1)
    three = jnp.roll(minus1, -1, axis=0)
    return jnp.stack([parts, plus1, two, three], axis=1)


def on_device(train_grads, query_grads, inverse_factors, repeat_counts):
    place = lax.axis_index("z")
    half = lax.axis_index("yh")
    first_half = half == 0
    query = query_grads[:, 0, :]
    roots = jnp.sqrt(repeat_counts.astype(jnp.float32))
    train = train_grads[:, 0, :] * roots[:, None]
    rows, width = train.shape
    quarter = width // 4
    total_rows = rows * lax.axis_size("z") * lax.axis_size("yh")

    own_rows = inverse_factors[0]
    swapped = swap_y(jnp.concatenate([train, own_rows]))
    other_train, other_rows = swapped[:rows], swapped[rows:]
    pair_rows = jnp.where(
        first_half,
        jnp.concatenate([own_rows, other_rows]),
        jnp.concatenate([other_rows, own_rows]),
    )
    inverse = lax.all_gather(pair_rows, "z", axis=0, tiled=True)

    plus1, minus1 = shift_z(query, -1), shift_z(query, 1)

    pair_train = jnp.where(
        first_half,
        jnp.concatenate([train, other_train]),
        jnp.concatenate([other_train, train]),
    )
    turned = jnp.where(first_half, pair_train, jnp.roll(pair_train, -quarter, axis=1))
    strip0 = dot(turned[:, :quarter], turned[:, : 3 * quarter], ((0,), (0,)))
    strip2 = dot(turned[:, 2 * quarter : 3 * quarter], turned[:, 2 * quarter :], ((0,), (0,)))
    partial = jnp.concatenate([strip0, strip2], axis=1)
    blocks, plus1, minus1 = lax.optimization_barrier(
        (partial.reshape(4, 4, quarter // 16, 5 * quarter), plus1, minus1)
    )
    plus2, minus2 = shift_z(plus1, -1), shift_z(minus1, 1)
    own_queries1 = jnp.concatenate([minus1, query, plus1])
    other_queries1 = swap_y(own_queries1)
    near_sums, plus2, minus2 = lax.optimization_barrier((reduce_near(blocks, place), plus2, minus2))
    own_queries2 = jnp.concatenate([minus2, plus2])
    part, other_queries1 = lax.optimization_barrier((reduce_far(near_sums, place), other_queries1))
    other_queries2 = swap_y(after(own_queries2, other_queries1))
    parts, inverse = lax.optimization_barrier((gather_far(part), inverse))
    gathered = gather_near(parts).reshape(quarter, 5 * quarter)
    strips = jnp.roll(gathered, place * (quarter // 16), axis=0)

    own_queries = jnp.concatenate([own_queries1, own_queries2])
    other_queries = jnp.concatenate([other_queries1, other_queries2])
    own_first = dot(own_queries, inverse, ((1,), (1,)))
    other_first = dot(other_queries, inverse, ((1,), (1,)))

    side = dot(pair_train, inverse, ((1,), (0,)))
    side_turned = jnp.where(first_half, side, jnp.roll(side, -quarter, axis=1))
    s0, s1, s2, s3 = (side_turned[:, i * quarter : (i + 1) * quarter] for i in range(4))
    b00, b01, b02, b22, b23 = (strips[:, i * quarter : (i + 1) * quarter] for i in range(5))
    straight0 = dot(s0, strips[:, : 3 * quarter], ((1,), (0,)))
    straight2 = dot(s2, strips[:, 3 * quarter :], ((1,), (0,)))
    crossed0 = dot(side_turned[:, quarter : 3 * quarter], strips[:, quarter : 3 * quarter], ((1,), (1,)))
    crossed2 = dot(s3, b23, ((1,), (1,)))
    product = jnp.concatenate(
        [
            straight0[:, :quarter] + crossed0,
            straight0[:, quarter : 2 * quarter],
            straight0[:, 2 * quarter :] + straight2[:, :quarter] + crossed2,
            straight2[:, quarter:],
        ],
        axis=1,
    )
    product = jnp.where(first_half, product, jnp.roll(product, quarter, axis=1))
    left = pair_train - (0.5 * DAMPING) * side - product * (1.0 / total_rows)

    own_scores = dot(left, own_first, ((1,), (1,)))
    other_scores = dot(left, other_first, ((1,), (1,)))
    even = jnp.where(first_half, own_scores, other_scores)
    odd = jnp.where(first_half, other_scores, own_scores)

    def tiles(scores, half_rows, offsets):
        at = (3, 0, 1, 2, 4)
        piece = scores[half_rows * rows : (half_rows + 1) * rows]
        return [piece[:, at[i] * rows : (at[i] + 1) * rows] for i in offsets]

    def mixed(first_tiles, second_tiles):
        out = []
        for i in range(9):
            out.append((first_tiles if i % 2 == 0 else second_tiles)[i // 2])
        return jnp.concatenate(out, axis=1)

    upper = mixed(tiles(even, 0, range(5)), tiles(odd, 0, range(4)))
    lower = mixed(tiles(odd, 1, range(5)), tiles(even, 1, range(1, 5)))
    upper, lower = lax.optimization_barrier((upper, lower))
    window = 9 * rows
    shares = lax.axis_size("yl") * lax.axis_size("x") * lax.axis_size("c")
    own = rows // shares
    terms = jnp.stack([upper, lower]).reshape(shares, 2, own, window)
    core = lax.axis_index("c")
    kept = lax.dynamic_index_in_dim(terms, core, 1, keepdims=False)
    sent = lax.dynamic_index_in_dim(terms, 1 - core, 1, keepdims=False)
    halves = kept + lax.ppermute(sent, "c", [(0, 1), (1, 0)])
    received = lax.all_to_all(halves.reshape(shares * own, window), ("yh", "yl", "x"), 0, 0, tiled=True)
    sums = received.reshape(shares, own, window).sum(axis=0)
    rank = lax.axis_index(("yl", "x", "c"))
    scale = lax.dynamic_slice_in_dim(roots, rank * own, own) * (1.0 / math.sqrt(width * shares))
    return sums * scale[:, None]


def solution(mesh):
    parts = Mesh(mesh.devices.reshape(16, 2, 2, 4, 2), ("z", "yh", "yl", "x", "c"))
    dp, layer = ("z", "yh"), ("yl", "x", "c")
    placed = (P(dp, layer, None), P(dp, layer, None), P(layer, dp, None), P(dp))
    return jax.shard_map(
        on_device, mesh=parts, in_specs=placed, out_specs=P(dp + layer, None), check_vma=False
    )
```

```python
import math

import jax
import jax.numpy as jnp
from jax import lax
from jax.sharding import Mesh, PartitionSpec as P

DAMPING = 0.5
FAST = lax.Precision.HIGH


def dot(left, right, dims):
    return lax.dot_general(
        left, right, (dims, ((), ())), precision=FAST, preferred_element_type=jnp.float32
    )


def shift_z(value, steps):
    count = lax.axis_size("z")
    return lax.ppermute(value, "z", [(i, (i + steps) % count) for i in range(count)])


def swap_y(value):
    return lax.ppermute(value, "yh", [(0, 1), (1, 0)])


def after(value, *others):
    return lax.optimization_barrier((value, *others))[0]


def reduce_near(blocks, place):
    def of_class(steps):
        return lax.dynamic_index_in_dim(blocks, (place + steps) % 4, 1, keepdims=False)

    opposite = of_class(2)
    from_left = shift_z(of_class(1), 1)
    from_right = shift_z(of_class(3), -1)
    from_left2 = shift_z(opposite[:, :8], 2)
    from_right2 = shift_z(opposite[:, 8:], -2)
    return of_class(0) + from_left + from_right + jnp.concatenate([from_left2, from_right2], axis=1)


def reduce_far(sums, place):
    row = place // 4

    def of_row(steps):
        return lax.dynamic_index_in_dim(sums, (row + steps) % 4, 0, keepdims=False)

    opposite = of_row(2)
    passing_right = shift_z(opposite[:8], 4)
    passing_left = shift_z(opposite[8:], -4)
    right, left = of_row(1), of_row(3)
    from_left = shift_z(jnp.concatenate([right[:8] + passing_right, right[8:]]), 4)
    from_right = shift_z(jnp.concatenate([left[:8], left[8:] + passing_left]), -4)
    return of_row(0) + from_left + from_right


def gather_far(part):
    plus4 = shift_z(part, -4)
    minus4 = shift_z(part, 4)
    plus8 = jnp.concatenate([shift_z(plus4[:8], -4), shift_z(minus4[8:], 4)])
    return jnp.stack([part, plus4, plus8, minus4])


def gather_near(parts):
    return (
        parts,
        shift_z(parts, -1),
        shift_z(parts, 1),
        shift_z(parts[:, :8], -2),
        shift_z(parts[:, 8:], 2),
    )


def joined(parts, plus1, minus1, plus2, minus2):
    two = jnp.concatenate([plus2, jnp.roll(minus2, -1, axis=0)], axis=1)
    three = jnp.roll(minus1, -1, axis=0)
    return jnp.stack([parts, plus1, two, three], axis=1)


def on_device(train_grads, query_grads, inverse_factors, repeat_counts):
    place = lax.axis_index("z")
    half = lax.axis_index("yh")
    first_half = half == 0
    query = query_grads[:, 0, :]
    roots = jnp.sqrt(repeat_counts.astype(jnp.float32))
    train = train_grads[:, 0, :] * roots[:, None]
    rows, width = train.shape
    quarter = width // 4
    total_rows = rows * lax.axis_size("z") * lax.axis_size("yh")

    own_rows = inverse_factors[0]
    swapped, plus1, minus1 = lax.optimization_barrier(
        (swap_y(jnp.concatenate([train, own_rows])), shift_z(query, -1), shift_z(query, 1))
    )
    other_train, other_rows = swapped[:rows], swapped[rows:]
    pair_rows = jnp.where(
        first_half,
        jnp.concatenate([own_rows, other_rows]),
        jnp.concatenate([other_rows, own_rows]),
    )
    inverse = lax.all_gather(pair_rows, "z", axis=0, tiled=True)

    pair_train = jnp.where(
        first_half,
        jnp.concatenate([train, other_train]),
        jnp.concatenate([other_train, train]),
    )
    turned = jnp.where(first_half, pair_train, jnp.roll(pair_train, -quarter, axis=1))
    strip0 = dot(turned[:, :quarter], turned[:, : 3 * quarter], ((0,), (0,)))
    strip2 = dot(turned[:, 2 * quarter : 3 * quarter], turned[:, 2 * quarter :], ((0,), (0,)))
    partial = jnp.concatenate([strip0, strip2], axis=1)
    blocks = partial.reshape(4, 4, quarter // 16, 5 * quarter)
    own_queries1 = jnp.concatenate([minus1, query, plus1])
    other_queries1 = swap_y(own_queries1)
    near_sums, plus1, minus1 = lax.optimization_barrier((reduce_near(blocks, place), plus1, minus1))
    plus2, minus2 = shift_z(plus1, -1), shift_z(minus1, 1)
    part, plus2, minus2, other_queries1 = lax.optimization_barrier(
        (reduce_far(near_sums, place), plus2, minus2, other_queries1)
    )
    own_queries2 = jnp.concatenate([minus2, plus2])
    other_queries2 = swap_y(own_queries2)
    parts, other_queries2 = lax.optimization_barrier((gather_far(part), other_queries2))
    own_queries = jnp.concatenate([own_queries1, own_queries2])
    other_queries = jnp.concatenate([other_queries1, other_queries2])
    own_first = dot(own_queries, inverse, ((1,), (1,)))
    other_first = dot(other_queries, inverse, ((1,), (1,)))

    side = dot(pair_train, inverse, ((1,), (0,)))
    pieces, side, own_first, other_first = lax.optimization_barrier(
        (gather_near(parts), side, own_first, other_first)
    )
    gathered = joined(*pieces).reshape(quarter, 5 * quarter)
    strips = jnp.roll(gathered, place * (quarter // 16), axis=0)
    side_turned = jnp.where(first_half, side, jnp.roll(side, -quarter, axis=1))
    s0, s1, s2, s3 = (side_turned[:, i * quarter : (i + 1) * quarter] for i in range(4))
    b00, b01, b02, b22, b23 = (strips[:, i * quarter : (i + 1) * quarter] for i in range(5))
    straight0 = dot(s0, strips[:, : 3 * quarter], ((1,), (0,)))
    straight2 = dot(s2, strips[:, 3 * quarter :], ((1,), (0,)))
    crossed0 = dot(side_turned[:, quarter : 3 * quarter], strips[:, quarter : 3 * quarter], ((1,), (1,)))
    crossed2 = dot(s3, b23, ((1,), (1,)))
    product = jnp.concatenate(
        [
            straight0[:, :quarter] + crossed0,
            straight0[:, quarter : 2 * quarter],
            straight0[:, 2 * quarter :] + straight2[:, :quarter] + crossed2,
            straight2[:, quarter:],
        ],
        axis=1,
    )
    product = jnp.where(first_half, product, jnp.roll(product, quarter, axis=1))
    left = pair_train - (0.5 * DAMPING) * side - product * (1.0 / total_rows)

    own_scores = dot(left, own_first, ((1,), (1,)))
    other_scores = dot(left, other_first, ((1,), (1,)))
    even = jnp.where(first_half, own_scores, other_scores)
    odd = jnp.where(first_half, other_scores, own_scores)

    def tiles(scores, half_rows, offsets):
        at = (3, 0, 1, 2, 4)
        piece = scores[half_rows * rows : (half_rows + 1) * rows]
        return [piece[:, at[i] * rows : (at[i] + 1) * rows] for i in offsets]

    def mixed(first_tiles, second_tiles):
        out = []
        for i in range(9):
            out.append((first_tiles if i % 2 == 0 else second_tiles)[i // 2])
        return jnp.concatenate(out, axis=1)

    upper = mixed(tiles(even, 0, range(5)), tiles(odd, 0, range(4)))
    lower = mixed(tiles(odd, 1, range(5)), tiles(even, 1, range(1, 5)))
    upper, lower = lax.optimization_barrier((upper, lower))
    window = 9 * rows
    shares = lax.axis_size("yl") * lax.axis_size("x") * lax.axis_size("c")
    own = rows // shares
    terms = jnp.stack([upper, lower]).reshape(shares, 2, own, window)
    core = lax.axis_index("c")
    kept = lax.dynamic_index_in_dim(terms, core, 1, keepdims=False)
    sent = lax.dynamic_index_in_dim(terms, 1 - core, 1, keepdims=False)
    halves = kept + lax.ppermute(sent, "c", [(0, 1), (1, 0)])
    received = lax.all_to_all(halves.reshape(shares * own, window), ("yh", "yl", "x"), 0, 0, tiled=True)
    sums = received.reshape(shares, own, window).sum(axis=0)
    rank = lax.axis_index(("yl", "x", "c"))
    scale = lax.dynamic_slice_in_dim(roots, rank * own, own) * (1.0 / math.sqrt(width * shares))
    return sums * scale[:, None]


def solution(mesh):
    parts = Mesh(mesh.devices.reshape(16, 2, 2, 4, 2), ("z", "yh", "yl", "x", "c"))
    dp, layer = ("z", "yh"), ("yl", "x", "c")
    placed = (P(dp, layer, None), P(dp, layer, None), P(layer, dp, None), P(dp))
    return jax.shard_map(
        on_device, mesh=parts, in_specs=placed, out_specs=P(dp + layer, None), check_vma=False
    )
```

```python
import math

import jax
import jax.numpy as jnp
from jax import lax
from jax.sharding import Mesh, PartitionSpec as P

DAMPING = 0.5
FAST = lax.Precision.HIGH


def dot(left, right, dims):
    return lax.dot_general(
        left, right, (dims, ((), ())), precision=FAST, preferred_element_type=jnp.float32
    )


def shift_z(value, steps):
    count = lax.axis_size("z")
    return lax.ppermute(value, "z", [(i, (i + steps) % count) for i in range(count)])


def swap_y(value):
    return lax.ppermute(value, "yh", [(0, 1), (1, 0)])


def after(value, *others):
    return lax.optimization_barrier((value, *others))[0]


def reduce_near(blocks, place):
    def of_class(steps):
        return lax.dynamic_index_in_dim(blocks, (place + steps) % 4, 1, keepdims=False)

    opposite = of_class(2)
    from_left = shift_z(of_class(1), 1)
    from_right = shift_z(of_class(3), -1)
    from_left2 = shift_z(opposite[:, :8], 2)
    from_right2 = shift_z(opposite[:, 8:], -2)
    return of_class(0) + from_left + from_right + jnp.concatenate([from_left2, from_right2], axis=1)


def reduce_far(sums, place):
    row = place // 4

    def of_row(steps):
        return lax.dynamic_index_in_dim(sums, (row + steps) % 4, 0, keepdims=False)

    from_left = shift_z(of_row(1), 4)
    from_right = shift_z(of_row(3), -4)
    across = shift_z(of_row(2), 8)
    return of_row(0) + from_left + from_right + across


def gather_far(part):
    return jnp.stack([part, shift_z(part, -4), shift_z(part, 8), shift_z(part, 4)])


def gather_near(parts):
    return (
        parts,
        shift_z(parts, -1),
        shift_z(parts, 1),
        shift_z(parts, -2),
    )


def joined(parts, plus1, minus1, two):
    three = jnp.roll(minus1, -1, axis=0)
    return jnp.stack([parts, plus1, two, three], axis=1)


def on_device(train_grads, query_grads, inverse_factors, repeat_counts):
    place = lax.axis_index("z")
    half = lax.axis_index("yh")
    first_half = half == 0
    query = query_grads[:, 0, :]
    roots = jnp.sqrt(repeat_counts.astype(jnp.float32))
    train = train_grads[:, 0, :] * roots[:, None]
    rows, width = train.shape
    quarter = width // 4
    total_rows = rows * lax.axis_size("z") * lax.axis_size("yh")

    own_rows = inverse_factors[0]
    swapped, plus1, minus1 = lax.optimization_barrier(
        (swap_y(jnp.concatenate([train, own_rows])), shift_z(query, -1), shift_z(query, 1))
    )
    other_train, other_rows = swapped[:rows], swapped[rows:]
    pair_rows = jnp.where(
        first_half,
        jnp.concatenate([own_rows, other_rows]),
        jnp.concatenate([other_rows, own_rows]),
    )
    inverse = lax.all_gather(pair_rows, "z", axis=0, tiled=True)

    pair_train = jnp.where(
        first_half,
        jnp.concatenate([train, other_train]),
        jnp.concatenate([other_train, train]),
    )
    turned = jnp.where(first_half, pair_train, jnp.roll(pair_train, -quarter, axis=1))
    strip0 = dot(turned[:, :quarter], turned[:, : 3 * quarter], ((0,), (0,)))
    strip2 = dot(turned[:, 2 * quarter : 3 * quarter], turned[:, 2 * quarter :], ((0,), (0,)))
    partial = jnp.concatenate([strip0, strip2], axis=1)
    blocks = partial.reshape(4, 4, quarter // 16, 5 * quarter)
    own_queries1 = jnp.concatenate([minus1, query, plus1])
    other_queries1 = swap_y(own_queries1)
    near_sums, plus1, minus1 = lax.optimization_barrier((reduce_near(blocks, place), plus1, minus1))
    plus2, minus2 = shift_z(plus1, -1), shift_z(minus1, 1)
    part, other_queries1 = lax.optimization_barrier((reduce_far(near_sums, place), other_queries1))
    parts, plus2, minus2 = lax.optimization_barrier((gather_far(part), plus2, minus2))
    own_queries2 = jnp.concatenate([minus2, plus2])
    other_queries2 = swap_y(own_queries2)

    def first(queries):
        return dot(queries, inverse, ((1,), (1,)))

    side = dot(pair_train, inverse, ((1,), (0,)))
    near_first = first(own_queries1), first(own_queries2), first(other_queries1)
    side, near_first, other_queries2 = lax.optimization_barrier((side, near_first, other_queries2))
    own_first, other_first = near_first[:2], (near_first[2], first(other_queries2))
    pieces, own_first, other_first = lax.optimization_barrier(
        (gather_near(parts), own_first, other_first)
    )
    gathered = joined(*pieces).reshape(quarter, 5 * quarter)
    strips = jnp.roll(gathered, place * (quarter // 16), axis=0)
    side_turned = jnp.where(first_half, side, jnp.roll(side, -quarter, axis=1))
    s0, s1, s2, s3 = (side_turned[:, i * quarter : (i + 1) * quarter] for i in range(4))
    b00, b01, b02, b22, b23 = (strips[:, i * quarter : (i + 1) * quarter] for i in range(5))
    straight0 = dot(s0, strips[:, : 3 * quarter], ((1,), (0,)))
    straight2 = dot(s2, strips[:, 3 * quarter :], ((1,), (0,)))
    crossed0 = dot(side_turned[:, quarter : 3 * quarter], strips[:, quarter : 3 * quarter], ((1,), (1,)))
    crossed2 = dot(s3, b23, ((1,), (1,)))
    product = jnp.concatenate(
        [
            straight0[:, :quarter] + crossed0,
            straight0[:, quarter : 2 * quarter],
            straight0[:, 2 * quarter :] + straight2[:, :quarter] + crossed2,
            straight2[:, quarter:],
        ],
        axis=1,
    )
    product = jnp.where(first_half, product, jnp.roll(product, quarter, axis=1))
    left = pair_train - (0.5 * DAMPING) * side - product * (1.0 / total_rows)

    own_scores = [dot(left, piece, ((1,), (1,))) for piece in own_first]
    other_scores = [dot(left, piece, ((1,), (1,))) for piece in other_first]
    even = [jnp.where(first_half, own, other) for own, other in zip(own_scores, other_scores)]
    odd = [jnp.where(first_half, other, own) for own, other in zip(own_scores, other_scores)]

    def tiles(scores, half_rows, offsets):
        at = ((1, 0), (0, 0), (0, 1), (0, 2), (1, 1))
        piece = [part[half_rows * rows : (half_rows + 1) * rows] for part in scores]
        return [piece[at[i][0]][:, at[i][1] * rows : (at[i][1] + 1) * rows] for i in offsets]

    def mixed(first_tiles, second_tiles):
        out = []
        for i in range(9):
            out.append((first_tiles if i % 2 == 0 else second_tiles)[i // 2])
        return jnp.concatenate(out, axis=1)

    upper = mixed(tiles(even, 0, range(5)), tiles(odd, 0, range(4)))
    lower = mixed(tiles(odd, 1, range(5)), tiles(even, 1, range(1, 5)))
    upper, lower = lax.optimization_barrier((upper, lower))
    window = 9 * rows
    shares = lax.axis_size("yl") * lax.axis_size("x") * lax.axis_size("c")
    own = rows // shares
    terms = jnp.stack([upper, lower]).reshape(shares, 2, own, window)
    core = lax.axis_index("c")
    kept = lax.dynamic_index_in_dim(terms, core, 1, keepdims=False)
    sent = lax.dynamic_index_in_dim(terms, 1 - core, 1, keepdims=False)
    halves = kept + lax.ppermute(sent, "c", [(0, 1), (1, 0)])
    received = lax.all_to_all(halves.reshape(shares * own, window), ("yh", "yl", "x"), 0, 0, tiled=True)
    sums = received.reshape(shares, own, window).sum(axis=0)
    rank = lax.axis_index(("yl", "x", "c"))
    scale = lax.dynamic_slice_in_dim(roots, rank * own, own) * (1.0 / math.sqrt(width * shares))
    return sums * scale[:, None]


def solution(mesh):
    parts = Mesh(mesh.devices.reshape(16, 2, 2, 4, 2), ("z", "yh", "yl", "x", "c"))
    dp, layer = ("z", "yh"), ("yl", "x", "c")
    placed = (P(dp, layer, None), P(dp, layer, None), P(layer, dp, None), P(dp))
    return jax.shard_map(
        on_device, mesh=parts, in_specs=placed, out_specs=P(dp + layer, None), check_vma=False
    )
```

```python
import math

import jax
import jax.numpy as jnp
from jax import lax
from jax.sharding import Mesh, PartitionSpec as P

DAMPING = 0.5
FAST = lax.Precision.HIGH


def dot(left, right, dims):
    return lax.dot_general(
        left, right, (dims, ((), ())), precision=FAST, preferred_element_type=jnp.float32
    )


def shift_z(value, steps):
    count = lax.axis_size("z")
    return lax.ppermute(value, "z", [(i, (i + steps) % count) for i in range(count)])


def swap_y(value):
    return lax.ppermute(value, "yh", [(0, 1), (1, 0)])


def after(value, *others):
    return lax.optimization_barrier((value, *others))[0]


def reduce_near(blocks, place):
    def of_class(steps):
        return lax.dynamic_index_in_dim(blocks, (place + steps) % 4, 1, keepdims=False)

    opposite = of_class(2)
    from_left = shift_z(of_class(1), 1)
    from_right = shift_z(of_class(3), -1)
    from_left2 = shift_z(opposite[:, :8], 2)
    from_right2 = shift_z(opposite[:, 8:], -2)
    return of_class(0) + from_left + from_right + jnp.concatenate([from_left2, from_right2], axis=1)


def reduce_far(sums, place):
    row = place // 4

    def of_row(steps):
        return lax.dynamic_index_in_dim(sums, (row + steps) % 4, 0, keepdims=False)

    from_left = shift_z(of_row(1), 4)
    from_right = shift_z(of_row(3), -4)
    across = shift_z(of_row(2), 8)
    return of_row(0) + from_left + from_right + across


def gather_far(part):
    return jnp.stack([part, shift_z(part, -4), shift_z(part, 8), shift_z(part, 4)])


def gather_near(parts):
    return (
        parts,
        shift_z(parts, -1),
        shift_z(parts, 1),
        shift_z(parts, -2),
    )


def joined(parts, plus1, minus1, two):
    three = jnp.roll(minus1, -1, axis=0)
    return jnp.stack([parts, plus1, two, three], axis=1)


def on_device(train_grads, query_grads, inverse_factors, repeat_counts):
    place = lax.axis_index("z")
    half = lax.axis_index("yh")
    first_half = half == 0
    query = query_grads[:, 0, :]
    roots = jnp.sqrt(repeat_counts.astype(jnp.float32))
    train = train_grads[:, 0, :] * roots[:, None]
    rows, width = train.shape
    quarter = width // 4
    total_rows = rows * lax.axis_size("z") * lax.axis_size("yh")

    own_inverse = lax.all_gather(inverse_factors[0], "z", axis=0)
    other_train, plus1, minus1 = lax.optimization_barrier(
        (swap_y(train), shift_z(query, -1), shift_z(query, 1))
    )
    pair_train = jnp.where(
        first_half,
        jnp.concatenate([train, other_train]),
        jnp.concatenate([other_train, train]),
    )
    turned = jnp.where(first_half, pair_train, jnp.roll(pair_train, -quarter, axis=1))
    strip0 = dot(turned[:, :quarter], turned[:, : 3 * quarter], ((0,), (0,)))
    strip2 = dot(turned[:, 2 * quarter : 3 * quarter], turned[:, 2 * quarter :], ((0,), (0,)))
    partial = jnp.concatenate([strip0, strip2], axis=1)
    blocks = partial.reshape(4, 4, quarter // 16, 5 * quarter)
    near_sums, plus1, minus1 = lax.optimization_barrier((reduce_near(blocks, place), plus1, minus1))
    plus2, minus2 = shift_z(plus1, -1), shift_z(minus1, 1)
    part, own_inverse = lax.optimization_barrier((reduce_far(near_sums, place), own_inverse))
    other_inverse = swap_y(own_inverse)
    pieces = gather_near(gather_far(part))
    inverse = jnp.where(
        first_half,
        jnp.stack([own_inverse, other_inverse], axis=1),
        jnp.stack([other_inverse, own_inverse], axis=1),
    ).reshape(width, width)
    side = dot(pair_train, inverse, ((1,), (0,)))

    gathered = joined(*pieces).reshape(quarter, 5 * quarter)
    strips = jnp.roll(gathered, place * (quarter // 16), axis=0)
    side_turned = jnp.where(first_half, side, jnp.roll(side, -quarter, axis=1))
    s0, s1, s2, s3 = (side_turned[:, i * quarter : (i + 1) * quarter] for i in range(4))
    b00, b01, b02, b22, b23 = (strips[:, i * quarter : (i + 1) * quarter] for i in range(5))
    straight0 = dot(s0, strips[:, : 3 * quarter], ((1,), (0,)))
    straight2 = dot(s2, strips[:, 3 * quarter :], ((1,), (0,)))
    crossed0 = dot(side_turned[:, quarter : 3 * quarter], strips[:, quarter : 3 * quarter], ((1,), (1,)))
    crossed2 = dot(s3, b23, ((1,), (1,)))
    product = jnp.concatenate(
        [
            straight0[:, :quarter] + crossed0,
            straight0[:, quarter : 2 * quarter],
            straight0[:, 2 * quarter :] + straight2[:, :quarter] + crossed2,
            straight2[:, quarter:],
        ],
        axis=1,
    )
    product = jnp.where(first_half, product, jnp.roll(product, quarter, axis=1))
    other_product = swap_y(product)
    queries = jnp.concatenate([minus1, query, plus1]), jnp.concatenate([minus2, plus2])
    first = [dot(piece, inverse, ((1,), (1,))) for piece in queries]
    left = 2.0 * pair_train - DAMPING * side - (product + other_product) * (1.0 / total_rows)
    inner, outer = (dot(left, piece, ((1,), (1,))) for piece in first)
    before, after_ = outer[:, :rows], outer[:, rows:]
    upper = jnp.concatenate([before[:rows], inner[:rows], after_[:rows]], axis=1)
    lower = [before[rows:], inner[rows:], after_[rows:]]
    lower = jnp.where(
        first_half,
        jnp.concatenate([lower[1], lower[2], lower[0]], axis=1),
        jnp.concatenate(lower, axis=1),
    )
    upper, lower = lax.optimization_barrier((upper, lower))
    received = lax.all_to_all(
        jnp.concatenate([upper, lower]), ("yh", "yl", "x", "c"), 0, 0, tiled=True
    )
    shares = lax.axis_size("yl") * lax.axis_size("x") * lax.axis_size("c")
    own = rows // shares
    sums = received.reshape(2, shares, own, 5 * rows).sum(axis=1)
    same = jnp.where(first_half, sums[0], sums[1]).reshape(own, 5, rows)
    cross = jnp.where(first_half, sums[1], sums[0]).reshape(own, 5, rows)
    window = 9 * rows
    scores = jnp.stack([same, cross], axis=2).reshape(own, 10 * rows)[:, :window]
    rank = lax.axis_index(("yl", "x", "c"))
    scale = lax.dynamic_slice_in_dim(roots, rank * own, own) * (1.0 / math.sqrt(width * shares))
    return scores * scale[:, None]


def solution(mesh):
    parts = Mesh(mesh.devices.reshape(16, 2, 2, 4, 2), ("z", "yh", "yl", "x", "c"))
    dp, layer = ("z", "yh"), ("yl", "x", "c")
    placed = (P(dp, layer, None), P(dp, layer, None), P(layer, dp, None), P(dp))
    return jax.shard_map(
        on_device, mesh=parts, in_specs=placed, out_specs=P(dp + layer, None), check_vma=False
    )
```

```python
import math

import jax
import jax.numpy as jnp
from jax import lax
from jax.sharding import Mesh, PartitionSpec as P

DAMPING = 0.5
FAST = lax.Precision.HIGH


def dot(left, right, dims):
    return lax.dot_general(
        left, right, (dims, ((), ())), precision=FAST, preferred_element_type=jnp.float32
    )


def shift_z(value, steps):
    count = lax.axis_size("z")
    return lax.ppermute(value, "z", [(i, (i + steps) % count) for i in range(count)])


def swap_y(value):
    return lax.ppermute(value, "yh", [(0, 1), (1, 0)])


def after(value, *others):
    return lax.optimization_barrier((value, *others))[0]


def reduce_near(blocks, place):
    def of_class(steps):
        return lax.dynamic_index_in_dim(blocks, (place + steps) % 4, 1, keepdims=False)

    opposite = of_class(2)
    from_left = shift_z(of_class(1), 1)
    from_right = shift_z(of_class(3), -1)
    from_left2 = shift_z(opposite[:, :8], 2)
    from_right2 = shift_z(opposite[:, 8:], -2)
    return of_class(0) + from_left + from_right + jnp.concatenate([from_left2, from_right2], axis=1)


def reduce_far(sums, place):
    row = place // 4

    def of_row(steps):
        return lax.dynamic_index_in_dim(sums, (row + steps) % 4, 0, keepdims=False)

    from_left = shift_z(of_row(1), 4)
    from_right = shift_z(of_row(3), -4)
    across = shift_z(of_row(2), 8)
    return of_row(0) + from_left + from_right + across


def gather_far(part):
    return jnp.stack([part, shift_z(part, -4), shift_z(part, 8), shift_z(part, 4)])


def gather_near(parts):
    return (
        parts,
        shift_z(parts, -1),
        shift_z(parts, 1),
        shift_z(parts, -2),
    )


def joined(parts, plus1, minus1, two):
    three = jnp.roll(minus1, -1, axis=0)
    return jnp.stack([parts, plus1, two, three], axis=1)


def on_device(train_grads, query_grads, inverse_factors, repeat_counts):
    place = lax.axis_index("z")
    half = lax.axis_index("yh")
    first_half = half == 0
    query = query_grads[:, 0, :]
    roots = jnp.sqrt(repeat_counts.astype(jnp.float32))
    train = train_grads[:, 0, :] * roots[:, None]
    rows, width = train.shape
    quarter = width // 4
    total_rows = rows * lax.axis_size("z") * lax.axis_size("yh")

    own_inverse = lax.all_gather(inverse_factors[0], "z", axis=0)
    other_train = swap_y(train)
    plus1, minus1 = shift_z(query, -1), shift_z(query, 1)
    pair_train = jnp.where(
        first_half,
        jnp.concatenate([train, other_train]),
        jnp.concatenate([other_train, train]),
    )
    turned = jnp.where(first_half, pair_train, jnp.roll(pair_train, -quarter, axis=1))
    strip0 = dot(turned[:, :quarter], turned[:, : 3 * quarter], ((0,), (0,)))
    strip2 = dot(turned[:, 2 * quarter : 3 * quarter], turned[:, 2 * quarter :], ((0,), (0,)))
    partial = jnp.concatenate([strip0, strip2], axis=1)
    blocks = partial.reshape(4, 4, quarter // 16, 5 * quarter)
    near_sums = reduce_near(blocks, place)
    part, own_inverse, plus1, minus1 = lax.optimization_barrier(
        (reduce_far(near_sums, place), own_inverse, plus1, minus1)
    )
    plus2, minus2 = shift_z(plus1, -1), shift_z(minus1, 1)
    other_inverse = swap_y(own_inverse)
    pieces = gather_near(gather_far(part))
    inverse = jnp.where(
        first_half,
        jnp.stack([own_inverse, other_inverse], axis=1),
        jnp.stack([other_inverse, own_inverse], axis=1),
    ).reshape(width, width)
    side = dot(pair_train, inverse, ((1,), (0,)))

    gathered = joined(*pieces).reshape(quarter, 5 * quarter)
    strips = jnp.roll(gathered, place * (quarter // 16), axis=0)
    side_turned = jnp.where(first_half, side, jnp.roll(side, -quarter, axis=1))
    s0, s1, s2, s3 = (side_turned[:, i * quarter : (i + 1) * quarter] for i in range(4))
    b00, b01, b02, b22, b23 = (strips[:, i * quarter : (i + 1) * quarter] for i in range(5))
    straight0 = dot(s0, strips[:, : 3 * quarter], ((1,), (0,)))
    straight2 = dot(s2, strips[:, 3 * quarter :], ((1,), (0,)))
    crossed0 = dot(side_turned[:, quarter : 3 * quarter], strips[:, quarter : 3 * quarter], ((1,), (1,)))
    crossed2 = dot(s3, b23, ((1,), (1,)))
    product = jnp.concatenate(
        [
            straight0[:, :quarter] + crossed0,
            straight0[:, quarter : 2 * quarter],
            straight0[:, 2 * quarter :] + straight2[:, :quarter] + crossed2,
            straight2[:, quarter:],
        ],
        axis=1,
    )
    product = jnp.where(first_half, product, jnp.roll(product, quarter, axis=1))
    other_product = swap_y(product)
    queries = jnp.concatenate([minus1, query, plus1]), jnp.concatenate([minus2, plus2])
    first = [dot(piece, inverse, ((1,), (1,))) for piece in queries]
    left = 2.0 * pair_train - DAMPING * side - (product + other_product) * (1.0 / total_rows)
    inner, outer = (dot(left, piece, ((1,), (1,))) for piece in first)
    before, after_ = outer[:, :rows], outer[:, rows:]
    upper = jnp.concatenate([before[:rows], inner[:rows], after_[:rows]], axis=1)
    lower = [before[rows:], inner[rows:], after_[rows:]]
    lower = jnp.where(
        first_half,
        jnp.concatenate([lower[1], lower[2], lower[0]], axis=1),
        jnp.concatenate(lower, axis=1),
    )
    upper, lower = lax.optimization_barrier((upper, lower))
    received = lax.all_to_all(
        jnp.concatenate([upper, lower]), ("yh", "yl", "x", "c"), 0, 0, tiled=True
    )
    shares = lax.axis_size("yl") * lax.axis_size("x") * lax.axis_size("c")
    own = rows // shares
    sums = received.reshape(2, shares, own, 5 * rows).sum(axis=1)
    same = jnp.where(first_half, sums[0], sums[1]).reshape(own, 5, rows)
    cross = jnp.where(first_half, sums[1], sums[0]).reshape(own, 5, rows)
    window = 9 * rows
    scores = jnp.stack([same, cross], axis=2).reshape(own, 10 * rows)[:, :window]
    rank = lax.axis_index(("yl", "x", "c"))
    scale = lax.dynamic_slice_in_dim(roots, rank * own, own) * (1.0 / math.sqrt(width * shares))
    return scores * scale[:, None]


def solution(mesh):
    parts = Mesh(mesh.devices.reshape(16, 2, 2, 4, 2), ("z", "yh", "yl", "x", "c"))
    dp, layer = ("z", "yh"), ("yl", "x", "c")
    placed = (P(dp, layer, None), P(dp, layer, None), P(layer, dp, None), P(dp))
    return jax.shard_map(
        on_device, mesh=parts, in_specs=placed, out_specs=P(dp + layer, None), check_vma=False
    )
```

```python
import math

import jax
import jax.numpy as jnp
from jax import lax
from jax.sharding import Mesh, PartitionSpec as P

DAMPING = 0.5
FAST = lax.Precision.HIGH


def dot(left, right, dims):
    return lax.dot_general(
        left, right, (dims, ((), ())), precision=FAST, preferred_element_type=jnp.float32
    )


def shift_z(value, steps):
    count = lax.axis_size("z")
    return lax.ppermute(value, "z", [(i, (i + steps) % count) for i in range(count)])


def swap_y(value):
    return lax.ppermute(value, "yh", [(0, 1), (1, 0)])


def after(value, *others):
    return lax.optimization_barrier((value, *others))[0]


def reduce_near(blocks, place):
    def of_class(steps):
        return lax.dynamic_index_in_dim(blocks, (place + steps) % 4, 1, keepdims=False)

    opposite = of_class(2)
    from_left = shift_z(of_class(1), 1)
    from_right = shift_z(of_class(3), -1)
    from_left2 = shift_z(opposite[:, :8], 2)
    from_right2 = shift_z(opposite[:, 8:], -2)
    return of_class(0) + from_left + from_right + jnp.concatenate([from_left2, from_right2], axis=1)


def reduce_far(sums, place):
    row = place // 4

    def of_row(steps):
        return lax.dynamic_index_in_dim(sums, (row + steps) % 4, 0, keepdims=False)

    from_left = shift_z(of_row(1), 4)
    from_right = shift_z(of_row(3), -4)
    across = shift_z(of_row(2), 8)
    return of_row(0) + from_left + from_right + across


def gather_far(part):
    return jnp.stack([part, shift_z(part, -4), shift_z(part, 8), shift_z(part, 4)])


def gather_near(parts):
    return (
        parts,
        shift_z(parts, -1),
        shift_z(parts, 1),
        shift_z(parts[:, :8], -2),
        shift_z(parts[:, 8:], 2),
    )


def joined(parts, plus1, minus1, plus2, minus2):
    two = jnp.concatenate([plus2, jnp.roll(minus2, -1, axis=0)], axis=1)
    three = jnp.roll(minus1, -1, axis=0)
    return jnp.stack([parts, plus1, two, three], axis=1)


def on_device(train_grads, query_grads, inverse_factors, repeat_counts):
    place = lax.axis_index("z")
    half = lax.axis_index("yh")
    first_half = half == 0
    query = query_grads[:, 0, :]
    roots = jnp.sqrt(repeat_counts.astype(jnp.float32))
    train = train_grads[:, 0, :] * roots[:, None]
    rows, width = train.shape
    quarter = width // 4
    total_rows = rows * lax.axis_size("z") * lax.axis_size("yh")

    own_inverse = lax.all_gather(inverse_factors[0], "z", axis=0)
    other_train, plus1, minus1 = lax.optimization_barrier(
        (swap_y(train), shift_z(query, -1), shift_z(query, 1))
    )
    pair_train = jnp.where(
        first_half,
        jnp.concatenate([train, other_train]),
        jnp.concatenate([other_train, train]),
    )
    turned = jnp.where(first_half, pair_train, jnp.roll(pair_train, -quarter, axis=1))
    strip0 = dot(turned[:, :quarter], turned[:, : 3 * quarter], ((0,), (0,)))
    strip2 = dot(turned[:, 2 * quarter : 3 * quarter], turned[:, 2 * quarter :], ((0,), (0,)))
    partial = jnp.concatenate([strip0, strip2], axis=1)
    blocks = partial.reshape(4, 4, quarter // 16, 5 * quarter)
    near_sums, plus1, minus1 = lax.optimization_barrier((reduce_near(blocks, place), plus1, minus1))
    part, own_inverse = lax.optimization_barrier((reduce_far(near_sums, place), own_inverse))
    other_inverse = swap_y(own_inverse)
    pieces = gather_near(gather_far(part))
    inverse = jnp.where(
        first_half,
        jnp.stack([own_inverse, other_inverse], axis=1),
        jnp.stack([other_inverse, own_inverse], axis=1),
    ).reshape(width, width)
    side = dot(pair_train, inverse, ((1,), (0,)))
    pieces, side = lax.optimization_barrier((pieces, side))

    gathered = joined(*pieces).reshape(quarter, 5 * quarter)
    strips = jnp.roll(gathered, place * (quarter // 16), axis=0)
    side_turned = jnp.where(first_half, side, jnp.roll(side, -quarter, axis=1))
    s0, s1, s2, s3 = (side_turned[:, i * quarter : (i + 1) * quarter] for i in range(4))
    b00, b01, b02, b22, b23 = (strips[:, i * quarter : (i + 1) * quarter] for i in range(5))
    straight0 = dot(s0, strips[:, : 3 * quarter], ((1,), (0,)))
    straight2 = dot(s2, strips[:, 3 * quarter :], ((1,), (0,)))
    crossed0 = dot(side_turned[:, quarter : 3 * quarter], strips[:, quarter : 3 * quarter], ((1,), (1,)))
    crossed2 = dot(s3, b23, ((1,), (1,)))
    product = jnp.concatenate(
        [
            straight0[:, :quarter] + crossed0,
            straight0[:, quarter : 2 * quarter],
            straight0[:, 2 * quarter :] + straight2[:, :quarter] + crossed2,
            straight2[:, quarter:],
        ],
        axis=1,
    )
    product = jnp.where(first_half, product, jnp.roll(product, quarter, axis=1))
    other_product = swap_y(product)
    plus1, minus1, product = lax.optimization_barrier((plus1, minus1, product))
    plus2, minus2 = shift_z(plus1, -1), shift_z(minus1, 1)
    queries = jnp.concatenate([minus1, query, plus1]), jnp.concatenate([minus2, plus2])
    first = [dot(piece, inverse, ((1,), (1,))) for piece in queries]
    left = 2.0 * pair_train - DAMPING * side - (product + other_product) * (1.0 / total_rows)
    inner, outer = (dot(left, piece, ((1,), (1,))) for piece in first)
    before, after_ = outer[:, :rows], outer[:, rows:]
    upper = jnp.concatenate([before[:rows], inner[:rows], after_[:rows]], axis=1)
    lower = [before[rows:], inner[rows:], after_[rows:]]
    lower = jnp.where(
        first_half,
        jnp.concatenate([lower[1], lower[2], lower[0]], axis=1),
        jnp.concatenate(lower, axis=1),
    )
    upper, lower = lax.optimization_barrier((upper, lower))
    received = lax.all_to_all(
        jnp.concatenate([upper, lower]), ("yh", "yl", "x", "c"), 0, 0, tiled=True
    )
    shares = lax.axis_size("yl") * lax.axis_size("x") * lax.axis_size("c")
    own = rows // shares
    sums = received.reshape(2, shares, own, 5 * rows).sum(axis=1)
    same = jnp.where(first_half, sums[0], sums[1]).reshape(own, 5, rows)
    cross = jnp.where(first_half, sums[1], sums[0]).reshape(own, 5, rows)
    window = 9 * rows
    scores = jnp.stack([same, cross], axis=2).reshape(own, 10 * rows)[:, :window]
    rank = lax.axis_index(("yl", "x", "c"))
    scale = lax.dynamic_slice_in_dim(roots, rank * own, own) * (1.0 / math.sqrt(width * shares))
    return scores * scale[:, None]


def solution(mesh):
    parts = Mesh(mesh.devices.reshape(16, 2, 2, 4, 2), ("z", "yh", "yl", "x", "c"))
    dp, layer = ("z", "yh"), ("yl", "x", "c")
    placed = (P(dp, layer, None), P(dp, layer, None), P(layer, dp, None), P(dp))
    return jax.shard_map(
        on_device, mesh=parts, in_specs=placed, out_specs=P(dp + layer, None), check_vma=False
    )
```

```python
import math

import jax
import jax.numpy as jnp
from jax import lax
from jax.sharding import Mesh, PartitionSpec as P

DAMPING = 0.5
FAST = lax.Precision.HIGH


def dot(left, right, dims):
    return lax.dot_general(
        left, right, (dims, ((), ())), precision=FAST, preferred_element_type=jnp.float32
    )


def shift_z(value, steps):
    count = lax.axis_size("z")
    return lax.ppermute(value, "z", [(i, (i + steps) % count) for i in range(count)])


def swap_y(value):
    return lax.ppermute(value, "yh", [(0, 1), (1, 0)])


def after(value, *others):
    return lax.optimization_barrier((value, *others))[0]


def reduce_near(blocks, place):
    def of_class(steps):
        return lax.dynamic_index_in_dim(blocks, (place + steps) % 4, 1, keepdims=False)

    opposite = of_class(2)
    from_left = shift_z(of_class(1), 1)
    from_right = shift_z(of_class(3), -1)
    from_left2 = shift_z(opposite[:, :8], 2)
    from_right2 = shift_z(opposite[:, 8:], -2)
    return of_class(0) + from_left + from_right + jnp.concatenate([from_left2, from_right2], axis=1)


def reduce_far(sums, place):
    row = place // 4

    def of_row(steps):
        return lax.dynamic_index_in_dim(sums, (row + steps) % 4, 0, keepdims=False)

    from_left = shift_z(of_row(1), 4)
    from_right = shift_z(of_row(3), -4)
    across = shift_z(of_row(2), 8)
    return of_row(0) + from_left + from_right + across


def gather_far(part):
    return jnp.stack([part, shift_z(part, -4), shift_z(part, 8), shift_z(part, 4)])


def gather_near(parts):
    return (
        parts,
        shift_z(parts, -1),
        shift_z(parts, 1),
        shift_z(parts[:, :8], -2),
        shift_z(parts[:, 8:], 2),
    )


def joined(parts, plus1, minus1, plus2, minus2):
    two = jnp.concatenate([plus2, jnp.roll(minus2, -1, axis=0)], axis=1)
    three = jnp.roll(minus1, -1, axis=0)
    return jnp.stack([parts, plus1, two, three], axis=1)


def on_device(train_grads, query_grads, inverse_factors, repeat_counts):
    place = lax.axis_index("z")
    half = lax.axis_index("yh")
    first_half = half == 0
    query = query_grads[:, 0, :]
    roots = jnp.sqrt(repeat_counts.astype(jnp.float32))
    train = train_grads[:, 0, :] * roots[:, None]
    rows, width = train.shape
    quarter = width // 4
    total_rows = rows * lax.axis_size("z") * lax.axis_size("yh")

    own_inverse = lax.all_gather(inverse_factors[0], "z", axis=0)
    other_train, plus1, minus1 = lax.optimization_barrier(
        (swap_y(train), shift_z(query, -1), shift_z(query, 1))
    )
    pair_train = jnp.where(
        first_half,
        jnp.concatenate([train, other_train]),
        jnp.concatenate([other_train, train]),
    )
    turned = jnp.where(first_half, pair_train, jnp.roll(pair_train, -quarter, axis=1))
    strip0 = dot(turned[:, :quarter], turned[:, : 3 * quarter], ((0,), (0,)))
    strip2 = dot(turned[:, 2 * quarter : 3 * quarter], turned[:, 2 * quarter :], ((0,), (0,)))
    partial = jnp.concatenate([strip0, strip2], axis=1)
    blocks = partial.reshape(4, 4, quarter // 16, 5 * quarter)
    halves = pair_train.reshape(2 * rows, width // 64, 2, 32)
    even, odd = (halves[:, :, i].reshape(2 * rows, width // 2) for i in range(2))
    own_half, other_half = jnp.where(first_half, even, odd), jnp.where(first_half, odd, even)
    near_sums, plus1, minus1, own_half, other_half = lax.optimization_barrier(
        (reduce_near(blocks, place), plus1, minus1, own_half, other_half)
    )
    part, own_inverse = lax.optimization_barrier((reduce_far(near_sums, place), own_inverse))
    other_inverse = swap_y(own_inverse)
    pieces = gather_near(gather_far(part))
    inverse = jnp.where(
        first_half,
        jnp.stack([own_inverse, other_inverse], axis=1),
        jnp.stack([other_inverse, own_inverse], axis=1),
    ).reshape(width, width)
    side = dot(own_half, own_inverse.reshape(width // 2, width), ((1,), (0,)))
    side = side + dot(other_half, other_inverse.reshape(width // 2, width), ((1,), (0,)))
    pieces, side = lax.optimization_barrier((pieces, side))

    gathered = joined(*pieces).reshape(quarter, 5 * quarter)
    strips = jnp.roll(gathered, place * (quarter // 16), axis=0)
    side_turned = jnp.where(first_half, side, jnp.roll(side, -quarter, axis=1))
    s0, s1, s2, s3 = (side_turned[:, i * quarter : (i + 1) * quarter] for i in range(4))
    b00, b01, b02, b22, b23 = (strips[:, i * quarter : (i + 1) * quarter] for i in range(5))
    straight0 = dot(s0, strips[:, : 3 * quarter], ((1,), (0,)))
    straight2 = dot(s2, strips[:, 3 * quarter :], ((1,), (0,)))
    crossed0 = dot(side_turned[:, quarter : 3 * quarter], strips[:, quarter : 3 * quarter], ((1,), (1,)))
    crossed2 = dot(s3, b23, ((1,), (1,)))
    product = jnp.concatenate(
        [
            straight0[:, :quarter] + crossed0,
            straight0[:, quarter : 2 * quarter],
            straight0[:, 2 * quarter :] + straight2[:, :quarter] + crossed2,
            straight2[:, quarter:],
        ],
        axis=1,
    )
    product = jnp.where(first_half, product, jnp.roll(product, quarter, axis=1))
    other_product = swap_y(product)
    plus1, minus1, product = lax.optimization_barrier((plus1, minus1, product))
    plus2, minus2 = shift_z(plus1, -1), shift_z(minus1, 1)
    queries = jnp.concatenate([minus1, query, plus1]), jnp.concatenate([minus2, plus2])
    first = [dot(piece, inverse, ((1,), (1,))) for piece in queries]
    left = 2.0 * pair_train - DAMPING * side - (product + other_product) * (1.0 / total_rows)
    inner, outer = (dot(left, piece, ((1,), (1,))) for piece in first)
    before, after_ = outer[:, :rows], outer[:, rows:]
    upper = jnp.concatenate([before[:rows], inner[:rows], after_[:rows]], axis=1)
    lower = [before[rows:], inner[rows:], after_[rows:]]
    lower = jnp.where(
        first_half,
        jnp.concatenate([lower[1], lower[2], lower[0]], axis=1),
        jnp.concatenate(lower, axis=1),
    )
    upper, lower = lax.optimization_barrier((upper, lower))
    received = lax.all_to_all(
        jnp.concatenate([upper, lower]), ("yh", "yl", "x", "c"), 0, 0, tiled=True
    )
    shares = lax.axis_size("yl") * lax.axis_size("x") * lax.axis_size("c")
    own = rows // shares
    sums = received.reshape(2, shares, own, 5 * rows).sum(axis=1)
    same = jnp.where(first_half, sums[0], sums[1]).reshape(own, 5, rows)
    cross = jnp.where(first_half, sums[1], sums[0]).reshape(own, 5, rows)
    window = 9 * rows
    scores = jnp.stack([same, cross], axis=2).reshape(own, 10 * rows)[:, :window]
    rank = lax.axis_index(("yl", "x", "c"))
    scale = lax.dynamic_slice_in_dim(roots, rank * own, own) * (1.0 / math.sqrt(width * shares))
    return scores * scale[:, None]


def solution(mesh):
    parts = Mesh(mesh.devices.reshape(16, 2, 2, 4, 2), ("z", "yh", "yl", "x", "c"))
    dp, layer = ("z", "yh"), ("yl", "x", "c")
    placed = (P(dp, layer, None), P(dp, layer, None), P(layer, dp, None), P(dp))
    return jax.shard_map(
        on_device, mesh=parts, in_specs=placed, out_specs=P(dp + layer, None), check_vma=False
    )
```

```python
import math

import jax
import jax.numpy as jnp
from jax import lax
from jax.sharding import Mesh, PartitionSpec as P

DAMPING = 0.5
FAST = lax.Precision.HIGH


def dot(left, right, dims):
    return lax.dot_general(
        left, right, (dims, ((), ())), precision=FAST, preferred_element_type=jnp.float32
    )


def shift_z(value, steps):
    count = lax.axis_size("z")
    return lax.ppermute(value, "z", [(i, (i + steps) % count) for i in range(count)])


def swap_y(value):
    return lax.ppermute(value, "yh", [(0, 1), (1, 0)])


def after(value, *others):
    return lax.optimization_barrier((value, *others))[0]


def reduce_near(blocks, place):
    def of_class(steps):
        return lax.dynamic_index_in_dim(blocks, (place + steps) % 4, 1, keepdims=False)

    opposite = of_class(2)
    from_left = shift_z(of_class(1), 1)
    from_right = shift_z(of_class(3), -1)
    from_left2 = shift_z(opposite[:, :8], 2)
    from_right2 = shift_z(opposite[:, 8:], -2)
    return of_class(0) + from_left + from_right + jnp.concatenate([from_left2, from_right2], axis=1)


def reduce_far(sums, place):
    row = place // 4

    def of_row(steps):
        return lax.dynamic_index_in_dim(sums, (row + steps) % 4, 0, keepdims=False)

    from_left = shift_z(of_row(1), 4)
    from_right = shift_z(of_row(3), -4)
    across = shift_z(of_row(2), 8)
    return of_row(0) + from_left + from_right + across


def gather_far(part):
    return jnp.stack([part, shift_z(part, -4), shift_z(part, 8), shift_z(part, 4)])


def gather_near(parts):
    return (
        parts,
        shift_z(parts, -1),
        shift_z(parts, 1),
        shift_z(parts[:, :8], -2),
        shift_z(parts[:, 8:], 2),
    )


def joined(parts, plus1, minus1, plus2, minus2):
    two = jnp.concatenate([plus2, jnp.roll(minus2, -1, axis=0)], axis=1)
    three = jnp.roll(minus1, -1, axis=0)
    return jnp.stack([parts, plus1, two, three], axis=1)


def on_device(train_grads, query_grads, inverse_factors, repeat_counts):
    place = lax.axis_index("z")
    half = lax.axis_index("yh")
    first_half = half == 0
    query = query_grads[:, 0, :]
    roots = jnp.sqrt(repeat_counts.astype(jnp.float32))
    train = train_grads[:, 0, :] * roots[:, None]
    rows, width = train.shape
    quarter = width // 4
    total_rows = rows * lax.axis_size("z") * lax.axis_size("yh")

    own_inverse = lax.all_gather(inverse_factors[0], "z", axis=0)
    other_train, plus1 = lax.optimization_barrier((swap_y(train), shift_z(query, -1)))
    minus1 = shift_z(query, 1)
    pair_train = jnp.where(
        first_half,
        jnp.concatenate([train, other_train]),
        jnp.concatenate([other_train, train]),
    )
    turned = jnp.where(first_half, pair_train, jnp.roll(pair_train, -quarter, axis=1))
    strip0 = dot(turned[:, :quarter], turned[:, : 3 * quarter], ((0,), (0,)))
    strip2 = dot(turned[:, 2 * quarter : 3 * quarter], turned[:, 2 * quarter :], ((0,), (0,)))
    partial = jnp.concatenate([strip0, strip2], axis=1)
    blocks = partial.reshape(4, 4, quarter // 16, 5 * quarter)
    near_sums, plus1, minus1 = lax.optimization_barrier((reduce_near(blocks, place), plus1, minus1))
    part, own_inverse = lax.optimization_barrier((reduce_far(near_sums, place), own_inverse))
    other_inverse = swap_y(own_inverse)
    pieces = gather_near(gather_far(part))
    inverse = jnp.where(
        first_half,
        jnp.stack([own_inverse, other_inverse], axis=1),
        jnp.stack([other_inverse, own_inverse], axis=1),
    ).reshape(width, width)
    side = dot(pair_train, inverse, ((1,), (0,)))
    pieces, side = lax.optimization_barrier((pieces, side))

    gathered = joined(*pieces).reshape(quarter, 5 * quarter)
    strips = jnp.roll(gathered, place * (quarter // 16), axis=0)
    side_turned = jnp.where(first_half, side, jnp.roll(side, -quarter, axis=1))
    s0, s1, s2, s3 = (side_turned[:, i * quarter : (i + 1) * quarter] for i in range(4))
    b00, b01, b02, b22, b23 = (strips[:, i * quarter : (i + 1) * quarter] for i in range(5))
    straight0 = dot(s0, strips[:, : 3 * quarter], ((1,), (0,)))
    straight2 = dot(s2, strips[:, 3 * quarter :], ((1,), (0,)))
    crossed0 = dot(side_turned[:, quarter : 3 * quarter], strips[:, quarter : 3 * quarter], ((1,), (1,)))
    crossed2 = dot(s3, b23, ((1,), (1,)))
    product = jnp.concatenate(
        [
            straight0[:, :quarter] + crossed0,
            straight0[:, quarter : 2 * quarter],
            straight0[:, 2 * quarter :] + straight2[:, :quarter] + crossed2,
            straight2[:, quarter:],
        ],
        axis=1,
    )
    product = jnp.where(first_half, product, jnp.roll(product, quarter, axis=1))
    other_product = swap_y(product)
    plus1, minus1, product = lax.optimization_barrier((plus1, minus1, product))
    plus2, minus2 = shift_z(plus1, -1), shift_z(minus1, 1)
    queries = jnp.concatenate([minus1, query, plus1]), jnp.concatenate([minus2, plus2])
    first = [dot(piece, inverse, ((1,), (1,))) for piece in queries]
    left = 2.0 * pair_train - DAMPING * side - (product + other_product) * (1.0 / total_rows)
    inner, outer = (dot(left, piece, ((1,), (1,))) for piece in first)
    before, after_ = outer[:, :rows], outer[:, rows:]
    upper = jnp.concatenate([before[:rows], inner[:rows], after_[:rows]], axis=1)
    lower = [before[rows:], inner[rows:], after_[rows:]]
    lower = jnp.where(
        first_half,
        jnp.concatenate([lower[1], lower[2], lower[0]], axis=1),
        jnp.concatenate(lower, axis=1),
    )
    upper, lower = lax.optimization_barrier((upper, lower))
    received = lax.all_to_all(
        jnp.concatenate([upper, lower]), ("yh", "yl", "x", "c"), 0, 0, tiled=True
    )
    shares = lax.axis_size("yl") * lax.axis_size("x") * lax.axis_size("c")
    own = rows // shares
    sums = received.reshape(2, shares, own, 5 * rows).sum(axis=1)
    same = jnp.where(first_half, sums[0], sums[1]).reshape(own, 5, rows)
    cross = jnp.where(first_half, sums[1], sums[0]).reshape(own, 5, rows)
    window = 9 * rows
    scores = jnp.stack([same, cross], axis=2).reshape(own, 10 * rows)[:, :window]
    rank = lax.axis_index(("yl", "x", "c"))
    scale = lax.dynamic_slice_in_dim(roots, rank * own, own) * (1.0 / math.sqrt(width * shares))
    return scores * scale[:, None]


def solution(mesh):
    parts = Mesh(mesh.devices.reshape(16, 2, 2, 4, 2), ("z", "yh", "yl", "x", "c"))
    dp, layer = ("z", "yh"), ("yl", "x", "c")
    placed = (P(dp, layer, None), P(dp, layer, None), P(layer, dp, None), P(dp))
    return jax.shard_map(
        on_device, mesh=parts, in_specs=placed, out_specs=P(dp + layer, None), check_vma=False
    )
```
